256 devices in a mesh: role: 2 (over z_hi), dp: 16 (over z_lo, y), tensor: 8 (over x, core).
Axes of the slice: x: 4, y: 4, z: 8 (z_hi: 2, z_lo: 4; z = z_hi * 4 + z_lo), core: 2. Of those that a mesh axis runs over, the one named last changes fastest.
Arguments:
- kv_weight: bfloat16 [2048, 8192], P(('role', 'dp'), 'tensor'), may hold values from -0.0625 to 0.0625
- kv_bias: bfloat16 [2048], P('tensor'), may hold values from -3 to 3
- norm_gain: bfloat16 [8192], P('tensor'), may hold values from 0.099609375 to 1.8984375
- page_states: bfloat16 [65536, 8192], P(('role', 'dp'), 'tensor'), may hold values from -1800 to 1800
- page_replica: int32 [512, 1], P(('role', 'dp')), may hold values from 0 to 15; in each aligned block of 16 rows (0 to 15, 16 to 31, ...) at most 2 rows name the same one
- page_pos: int32 [512], P(('role', 'dp')), may hold values from 0 to 255
- page_fill: int32 [512], P(('role', 'dp')), may hold values from 1 to 128
- learn_normed: bfloat16 [8192, 8192], P(('role', 'dp'), 'tensor'), may hold values from -6 to 6
- learn_cot: bfloat16 [8192, 2048], P(('role', 'dp')), may hold values from -2.5 to 2.5
Outputs:
- kv_cache: bfloat16 [1024, 128, 2048], P(('role', 'dp'), None, 'tensor')
- normed_grad: bfloat16 [8192, 8192], P(('role', 'dp'), 'tensor')
- weight_grad: float32 [2048, 8192], P(('role', 'dp'), 'tensor')
The draws below stay inside these ranges and needn't reach their ends.
Inputs may be any that keep to these rules, and one draw needn't show every extreme that they name: `page_replica`: within the 16 pages of one device, at most 2 name the same replica.
All inputs are finite; a program needn't handle non-finite values.
Results may differ from the reference program's by a relative error of at most 0.022.
Values may be sent and summed in bfloat16 or wider, within the bound.
No kernel may reach another device: no remote copies, remote signals or barrier semaphores. Data moves between devices by JAX's collectives and lax.ppermute only.
A program may use at most 128 MiB of HBM per device.

```python
import math
import jax
import jax.numpy as jnp
import numpy as np
from jax import lax

D = 8192
KVH = 8
HD = 128
PAGE = 128
MAXP = 256
PAGES_DEV = 16
LTOK_DEV = 256
KVW = 2048
CAP = 2
SLOTS = 32
NPAGE = 512
LTOK = 8192
N_ROLE = 2
N_DP = 16


def draw_page_states(key, part):
    key = jax.random.fold_in(key, 11)
    key_base, key_rows, key_cols = jax.random.split(key, 3)
    row_count = NPAGE * PAGE
    row_scale = jnp.exp(jax.random.uniform(key_rows, (row_count, 1), jnp.float32, 0.0, math.log(10.0)))
    column_trend = jnp.exp(math.log(3.0) * jnp.arange(D, dtype=jnp.float32) / D)
    column_scale = jnp.exp(jax.random.uniform(key_cols, (1, D), jnp.float32, 0.0, math.log(10.0))) * column_trend[None, :]
    base_values = jnp.clip(jax.random.normal(key_base, (row_count, D), jnp.float32), -6.0, 6.0)
    return (base_values * row_scale * column_scale).astype(jnp.bfloat16)


def set_ends(values, rng, low, largest):
    spot = [jax.random.randint(jax.random.fold_in(rng, axis), (), 0, length) for axis, length in enumerate(values.shape)]
    main_axis = values.shape.index(max(values.shape))
    beside = spot[:main_axis] + [(spot[main_axis] + 1) % values.shape[main_axis]] + spot[main_axis + 1:]
    return values.at[tuple(spot)].set(low).at[tuple(beside)].set(largest)


def strengthened(values, key, source, target, blocks, factor):
    def block_of(dim):
        return (jnp.arange(values.shape[dim]) // (values.shape[dim] // blocks)).reshape((-1,) + (1,) * (values.ndim - 1 - dim))

    near = jax.random.permutation(key, blocks)[block_of(target)]
    far = (block_of(target) + blocks // 2) % blocks
    return jnp.where((block_of(source) == near) | (block_of(source) == far), factor * values, values)


def block_levels(key, dims, pieces, low, largest):
    level, own = 1.0, jax.random.fold_in(key, 6)
    for dim, parts in pieces:
        draws = jnp.exp(jax.random.uniform(jax.random.fold_in(own, dim), (parts,), jnp.float32, low / len(pieces), largest / len(pieces)))
        level = level * jnp.repeat(draws, dims[dim] // parts).reshape([-1 if axis == dim else 1 for axis in range(len(dims))])
    return level


def deal_out(stream_key, own, number, rows, count, top, limit, skew):
    ranking = jax.random.permutation(stream_key, count)
    crowded, common = load_shares(count, rows * top, limit, skew, True), load_shares(count, rows * top, limit, skew, False)
    places = jnp.arange(count)

    def named(tallies, offset_by):
        used = int((tallies > 0).sum())
        fixed = max(1, used // 4)
        shifted = fixed + (places - fixed + offset_by * (used - fixed)) % max(1, count - fixed)
        return jnp.zeros((count,), jnp.int32).at[ranking[jnp.where(places < fixed, places, shifted)]].set(jnp.asarray(tallies, jnp.int32))

    tallies = jnp.where(number % 4 == 0, named(crowded, number // 4), named(common, number - number // 4 - 1))
    mixed = jax.random.permutation(jax.random.fold_in(own, 3), count)
    donor, receiver = mixed[0:count // 2 * 2:2], mixed[1:count // 2 * 2:2]
    margin = jnp.minimum(tallies[donor] - 1, limit - tallies[receiver]) // 2
    margin = jnp.where((donor == ranking[0]) | (receiver == ranking[0]) | (tallies[receiver] == 0), 0, jnp.maximum(margin, 0))
    shifted = jax.random.randint(jax.random.fold_in(own, 4), (count // 2,), 0, 1 << 20) % (margin + 1)
    tallies = tallies.at[donor].add(-shifted).at[receiver].add(shifted)
    labels = jnp.searchsorted(jnp.cumsum(tallies), jnp.arange(rows * top), side="right").astype(jnp.int32)
    table = labels.reshape(top, rows).T
    table = table[jax.random.permutation(jax.random.fold_in(own, 1), rows)]
    offset_by = jax.random.randint(jax.random.fold_in(own, 2), (rows, 1), 0, top)
    return jnp.take_along_axis(table, (jnp.arange(top)[None, :] + offset_by) % top, axis=1)


def load_shares(number_of, total, reach, lean, full):
    weights = [(1 << 20) // math.isqrt(rank ** lean) + 1 for rank in range(1, number_of + 1)]
    largest = reach if full else min(reach, max(-(-total // number_of), total * weights[0] // sum(weights)))
    least = 1 if total - largest >= number_of - 1 else 0
    holding, surplus = [largest] + [least] * (number_of - 1), total - largest - least * (number_of - 1)
    while surplus > 0:
        free = [i for i in range(1, number_of) if holding[i] < largest] or [i for i in range(1, number_of) if holding[i] < reach]
        whole, remaining = sum([weights[i] for i in free]), surplus
        for i in free:
            addition = min(reach - holding[i], max(1, remaining * weights[i] // whole), surplus)
            holding[i] = holding[i] + addition
            surplus = surplus - addition
    return np.array(holding)


def noise(stream_key, extent, scale, bound, cuts=(), held_as=jnp.bfloat16):
    loudness = block_levels(stream_key, extent, cuts, -0.22, 0.18) if cuts else 1.0
    values = jax.random.normal(stream_key, extent, jnp.float32) * scale * loudness
    return jnp.minimum(jnp.maximum(values, -bound), bound).astype(held_as)


def heavy_noise(own_key, extent, scale, limit, pieces, heavy, kind=jnp.bfloat16):
    values = scale * jax.random.normal(own_key, extent, jnp.float32)
    if pieces:
        values = values * block_levels(own_key, extent, pieces, -0.22, 0.18)
    return jnp.clip(strengthened(values, jax.random.fold_in(own_key, 3), *heavy), -limit, limit).astype(kind)


def setup_inputs(seed: int = 0) -> dict:
    keys = jax.random.split(jax.random.key(seed), 10)
    kv_weight = noise(keys[0], (KVW, D), D ** -0.5, 0.0625, ((0, 32), (1, 8)))
    kv_bias = noise(keys[1], (KVW,), 0.5, 3.0, ((0, 8),))
    norm_gain = jnp.clip(1.0 + 0.18 * jax.random.normal(keys[2], (D,), jnp.float32), 0.099609375, 1.8984375).astype(jnp.bfloat16)
    page_states = draw_page_states(jax.random.fold_in(keys[9], 71), 0)
    page_replica_keys = jax.random.split(jax.random.fold_in(keys[4], 1), NPAGE // PAGES_DEV)
    page_replica_turns = jax.random.permutation(jax.random.fold_in(keys[4], 3), NPAGE // PAGES_DEV)
    page_replica = jax.vmap(lambda own, number: deal_out(jax.random.fold_in(keys[4], 2), own, number, PAGES_DEV, N_DP, 1, CAP, 2))(page_replica_keys, page_replica_turns).reshape((NPAGE, 1))
    page_pos = set_ends(jax.random.randint(keys[5], (NPAGE,), 0, MAXP), jax.random.fold_in(keys[5], 1), 0, MAXP - 1).astype(jnp.int32)
    page_fill = set_ends(jax.random.randint(keys[6], (NPAGE,), 1, PAGE + 1), jax.random.fold_in(keys[6], 1), 1, PAGE).astype(jnp.int32)
    learn_normed = noise(keys[7], (LTOK, D), 1.0, 6.0, ((0, 32), (1, 8)))
    learn_cot = heavy_noise(keys[8], (LTOK, KVW), 0.088, 2.5, ((0, 32),), (0, 1, 32, 2.75))
    return dict(kv_weight=kv_weight, kv_bias=kv_bias, norm_gain=norm_gain, page_states=page_states, page_replica=page_replica, page_pos=page_pos, page_fill=page_fill, learn_normed=learn_normed, learn_cot=learn_cot)


EPSILON = 1e-06
ROPE_BASE = 1000000.0

def rotate_keys(fresh_kv, positions):
    head_size = fresh_kv.shape[-1]
    half_size = head_size // 2
    exponent = jnp.arange(half_size, dtype=jnp.float32) * (2.0 / head_size)
    frequency = jnp.power(jnp.float32(ROPE_BASE), -exponent)
    angles = positions.astype(jnp.float32)[:, None] * frequency[None, :]
    cosine = jnp.cos(angles)[:, None, :]
    sine_part = jnp.sin(angles)[:, None, :]
    key_part = fresh_kv[:, :, 0, :]
    first_half = key_part[..., :half_size]
    second_half = key_part[..., half_size:]
    turned = jnp.concatenate([first_half * cosine - second_half * sine_part, second_half * cosine + first_half * sine_part], axis=-1)
    return jnp.stack([turned, fresh_kv[:, :, 1, :]], axis=2)

def reference(kv_weight, kv_bias, norm_gain, page_states, page_replica, page_pos, page_fill, learn_normed, learn_cot):
    groups = N_ROLE * N_DP
    kv_width = kv_weight.shape[0]
    row_count = page_states.shape[0]
    widened = page_states.astype(jnp.float32)
    row_squares = lax.optimization_barrier(jnp.sum(widened * widened, axis=1))
    scaled = (widened * norm_gain.astype(jnp.float32)[None, :]).astype(jnp.bfloat16)
    projected = jnp.dot(scaled, kv_weight.T, preferred_element_type=jnp.float32)
    fresh_kv = projected * lax.rsqrt(row_squares / D + EPSILON)[:, None] + kv_bias.astype(jnp.float32)[None, :]
    offsets = jnp.arange(PAGE, dtype=jnp.int32)
    positions = (page_pos[:, None] * PAGE + offsets[None, :]).reshape(-1)
    turned = rotate_keys(fresh_kv.reshape(row_count, KVH, 2, HD), positions)
    live_rows = (offsets[None, :] < page_fill[:, None]).reshape(-1)
    kv_pages = jnp.where(live_rows[:, None], turned.reshape(row_count, kv_width), 0.0).astype(jnp.bfloat16)
    owners = page_replica[:, 0].reshape(groups, PAGES_DEV)
    same_owner = owners[:, :, None] == owners[:, None, :]
    earlier = jnp.arange(PAGES_DEV)[None, :] < jnp.arange(PAGES_DEV)[:, None]
    page_rank = lax.optimization_barrier(jnp.sum(jnp.where(same_owner & earlier[None, :, :], 1, 0), axis=2)).astype(jnp.int32)
    group_ids = jnp.arange(groups, dtype=jnp.int32)[:, None]
    role_ids = group_ids // N_DP
    replica_ids = group_ids % N_DP
    target = (role_ids * N_DP + owners) * SLOTS + replica_ids * CAP + page_rank
    kv_cache = jnp.zeros((groups * SLOTS, PAGE, kv_width), jnp.bfloat16)
    kv_cache = kv_cache.at[target.reshape(-1).astype(jnp.int32)].set(kv_pages.reshape(-1, PAGE, kv_width))
    normed_grad = jnp.dot(learn_cot, kv_weight, preferred_element_type=jnp.float32).astype(jnp.bfloat16)
    cot_groups = learn_cot.reshape(groups, LTOK_DEV, kv_width)
    normed_groups = learn_normed.reshape(groups, LTOK_DEV, D)

    def add_group(running, operands):
        cot_rows, normed_rows = operands
        grad_part = jnp.dot(cot_rows.T, normed_rows, preferred_element_type=jnp.float32).astype(jnp.bfloat16)
        grad_part = lax.optimization_barrier(grad_part)
        return (running + grad_part.astype(jnp.float32), None)
    weight_grad, _ = lax.scan(add_group, jnp.zeros((kv_width, D), jnp.float32), (cot_groups, normed_groups))
    return (kv_cache, normed_grad, weight_grad)
```

```python
import jax
import jax.numpy as jnp
from jax import lax
from jax.experimental import pallas as pl
from jax.experimental.pallas import tpu as pltpu
from jax.sharding import Mesh, PartitionSpec as P

HD = 128
PAGE = 128
EPSILON = 1e-06
ROPE_BASE = 1000000.0

Z = ("role", "zl")
ROWS = ("role", "zl", "y")
DP = ("zl", "y")
TENSOR = ("x", "core")

CHUNKS = ((0, 64), (64, 64))
F32 = jnp.float32
BF16 = jnp.bfloat16


def ring(size, step):
    return [(i, (i + step) % size) for i in range(size)]


def shift(value, axis, size, step):
    return lax.ppermute(value, axis, ring(size, step))


def after(value, *earlier):
    return lax.optimization_barrier((value, earlier))[0]


def by_index(blocks, index):
    size = len(blocks)
    twice = jnp.stack(blocks + blocks[:-1])
    return lax.dynamic_slice_in_dim(twice, (size - index) % size, size, 0)


def unwritten(shape, dtype):
    return pl.pallas_call(
        lambda out_ref: None,
        out_specs=pl.BlockSpec(memory_space=pl.ANY),
        out_shape=jax.ShapeDtypeStruct(shape, dtype),
    )()


def gather_weight(weight):
    ny, y = lax.axis_size("y"), lax.axis_index("y")
    line = by_index([weight] + [shift(weight, "y", ny, -s) for s in range(1, ny)], y)
    line = line.reshape(-1, weight.shape[1])
    return lax.all_gather(line, Z, axis=0, tiled=False), line


def dot_rows(scaled_ref, weight_ref, rows):
    return lax.dot_general(
        scaled_ref[...].reshape(rows, scaled_ref.shape[2]), weight_ref[0], (((1,), (1,)), ((), ())),
        preferred_element_type=F32,
    )


def project_kernel(place_ref, scaled_ref, weight_ref, out_ref):
    out_ref[0] = dot_rows(scaled_ref, weight_ref, out_ref.shape[1]).astype(BF16)


def project_add_kernel(place_ref, scaled_ref, weight_ref, other_ref, *out_refs):
    rows = other_ref.shape[1]
    total = dot_rows(scaled_ref, weight_ref, rows) + other_ref[0].astype(F32)
    for step, out_ref in enumerate(out_refs):
        @pl.when(pl.program_id(0) == step)
        def _(out_ref=out_ref):
            out_ref[...] = total.astype(BF16)


def project(scaled, weight, place, chunk, other=None):
    pages, page, depth = scaled.shape
    heads, cols, _ = weight.shape
    heads //= 2
    start, part = chunk
    rows = pages * part

    def head(h, place_ref):
        return lax.rem(place_ref[0] + h, heads)

    specs = [
        pl.BlockSpec((pages, part, depth), lambda h, place_ref: (0, start // part, 0)),
        pl.BlockSpec((1, cols, depth), lambda h, place_ref: (2 * head(h, place_ref) + place_ref[1], 0, 0)),
    ]
    args = [scaled, weight]
    if other is None:
        out_specs = pl.BlockSpec((1, rows, cols), lambda h, place_ref: (head(h, place_ref), 0, 0))
        out_shape = jax.ShapeDtypeStruct((heads, rows, cols), BF16)
    else:
        specs.append(pl.BlockSpec((1, rows, cols), lambda h, place_ref: (head(h, place_ref), 0, 0)))
        args.append(other)
        out_specs = [pl.BlockSpec((rows, cols), lambda h, place_ref: (0, 0))] * heads
        out_shape = [jax.ShapeDtypeStruct((rows, cols), BF16)] * heads
    return pl.pallas_call(
        project_kernel if other is None else project_add_kernel,
        grid_spec=pltpu.PrefetchScalarGridSpec(
            num_scalar_prefetch=1, grid=(heads,), in_specs=specs, out_specs=out_specs
        ),
        out_shape=out_shape,
        compiler_params=pltpu.CompilerParams(vmem_limit_bytes=24 * 2**20),
        cost_estimate=pl.CostEstimate(
            flops=2 * rows * depth * cols * heads,
            bytes_accessed=2 * (rows * depth + heads * cols * (depth + rows)),
            transcendentals=0,
        ),
    )(place, *args)


def finish(parts, inverse, cosine, sine, bias, target, fill, chunk, slots):
    sources = len(parts)
    pages, part, cols = parts[0].shape
    group = 4
    start = chunk[0]

    def kernel(target_ref, fill_ref, inverse_ref, cosine_ref, sine_ref, bias_ref, *refs):
        part_refs, out_ref = refs[:-1], refs[-1]
        step = pl.program_id(0)

        @pl.when(step == 0)
        def _():
            out_ref[...] = jnp.zeros_like(out_ref)

        bias_row = bias_ref[...].astype(F32)
        offset = lax.broadcasted_iota(jnp.int32, (part, HD), 0) + start
        for i in range(group):
            page = step * group + i
            total = part_refs[0][i].astype(F32)
            for part_ref in part_refs[1:]:
                total = total + part_ref[i].astype(F32)
            scale = inverse_ref[i]
            key = total[:, :HD] * scale + bias_row[:, :HD]
            value = total[:, HD:] * scale + bias_row[:, HD:]
            key = key * cosine_ref[i] + pltpu.roll(key, HD // 2, 1) * sine_ref[i]
            live = offset < fill_ref[page]
            where = target_ref[page]
            out_ref[where, :, :HD] = jnp.where(live, key, 0.0).astype(BF16)
            out_ref[where, :, HD:] = jnp.where(live, value, 0.0).astype(BF16)

    table = pl.BlockSpec((group, part, HD), lambda g, *_: (g, start // part, 0))
    return pl.pallas_call(
        kernel,
        grid_spec=pltpu.PrefetchScalarGridSpec(
            num_scalar_prefetch=2,
            grid=(pages // group,),
            in_specs=[
                table,
                table,
                table,
                pl.BlockSpec((1, cols), lambda g, *_: (0, 0)),
            ]
            + [pl.BlockSpec((group, part, cols), lambda g, *_: (g, 0, 0))] * sources,
            out_specs=pl.BlockSpec((slots, part, cols), lambda g, *_: (0, 0, 0)),
        ),
        out_shape=jax.ShapeDtypeStruct((slots, part, cols), BF16),
        compiler_params=pltpu.CompilerParams(vmem_limit_bytes=48 * 2**20),
        cost_estimate=pl.CostEstimate(
            flops=12 * pages * part * cols,
            bytes_accessed=2 * part * cols * (sources * pages + slots) + 12 * pages * part * HD,
            transcendentals=0,
        ),
    )(target, fill, inverse, cosine, sine, bias, *parts)


def shards(
    kv_weight,
    kv_bias,
    norm_gain,
    page_states,
    page_replica,
    page_pos,
    page_fill,
    learn_normed,
    learn_cot,
):
    nz, ny, nx = lax.axis_size(Z), lax.axis_size("y"), lax.axis_size("x")
    core, x, y, z = (lax.axis_index(name) for name in ("core", "x", "y", Z))
    pages = page_fill.shape[0]
    depth = page_states.shape[1]
    feature_count = depth * lax.axis_size(TENSOR)
    rows = kv_weight.shape[0]

    tokens = learn_cot.shape[0]
    half = HD // 2
    replicas = lax.axis_size(DP)
    capacity = max(2, 2 * pages // replicas)
    slots = replicas * capacity

    weight, line = gather_weight(kv_weight)

    cot = after(learn_cot, line).reshape(tokens, nz, ny, rows).transpose(0, 2, 1, 3)
    terms = lax.dot_general(
        cot.reshape(tokens, -1), learn_normed, (((0,), (0,)), ((), ())), preferred_element_type=F32
    ).astype(BF16)
    terms = lax.psum_scatter(terms, "y", scatter_dimension=0, tiled=True)

    states, gain, place, owners = after(
        (page_states, norm_gain, page_pos, page_replica[:, 0]), line
    )
    widened = states.astype(F32)
    scaled = (widened * gain.astype(F32)[None, :]).astype(BF16).reshape(pages, PAGE, depth)
    squares = jnp.sum(widened * widened, axis=1).reshape(pages, PAGE)
    squares = squares + shift(squares, "core", 2, 1)
    squares = squares + shift(squares, "x", nx, 1) + shift(squares, "x", nx, 2) + shift(squares, "x", nx, 3)
    inverse = lax.rsqrt(squares / feature_count + EPSILON)
    inverse = jnp.broadcast_to(inverse[:, :, None], (pages, PAGE, HD))

    exponent = jnp.arange(half, dtype=F32) * (2.0 / HD)
    frequency = jnp.power(F32(ROPE_BASE), -exponent)
    positions = place[:, None] * PAGE + jnp.arange(PAGE, dtype=jnp.int32)[None, :]
    angles = positions.astype(F32)[:, :, None] * frequency[None, None, :]
    cosine, sine = jnp.cos(angles), jnp.sin(angles)
    cosine = jnp.concatenate([cosine, cosine], axis=2)
    sine = jnp.concatenate([-sine, sine], axis=2)

    earlier = jnp.arange(pages)[None, :] < jnp.arange(pages)[:, None]
    same = owners[:, None] == owners[None, :]
    rank = jnp.sum(jnp.where(same & earlier, 1, 0), axis=1).astype(jnp.int32)
    target = owners * capacity + rank

    weight, scaled, inverse, cosine, sine, target = lax.optimization_barrier(
        (weight, scaled, inverse, cosine, sine, target)
    )
    weight_grad = lax.psum_scatter(terms, Z, scatter_dimension=0, tiled=True).astype(F32)

    own, far = jnp.stack([x, core]), jnp.stack([x, 1 - core])
    mine = []
    away = [shift(project(scaled, weight, far, chunk), "core", 2, 1) for chunk in CHUNKS[:2]]
    for c, chunk in enumerate(CHUNKS):
        mine.append(project(scaled, weight, own, chunk, away[c]))
        if c + 2 < len(CHUNKS):
            scaled = after(scaled, mine[c])
            away.append(shift(project(scaled, weight, far, CHUNKS[c + 2]), "core", 2, 1))

    kv_cache = unwritten((slots, PAGE, 2 * HD), BF16)
    for c, chunk in enumerate(CHUNKS):
        start, part = chunk
        parts = [m if s == 0 else shift(m, "x", nx, s) for s, m in enumerate(mine[c])]
        parts = [p.reshape(pages, part, 2 * HD) for p in parts]
        placed = finish(
            parts, inverse, cosine, sine, kv_bias[None, :], target, page_fill, chunk, slots
        )
        if c == 0:
            placed = after(placed, mine[-1], weight_grad)
        else:
            placed = after(placed, piece)
        piece = lax.all_to_all(placed, DP, 0, 0, tiled=True)
        kv_cache = lax.dynamic_update_slice(kv_cache, piece, (0, start, 0))

    learn_cot, _ = lax.optimization_barrier((learn_cot, placed))
    normed_grad = jnp.dot(
        learn_cot, weight.reshape(-1, depth), preferred_element_type=F32
    ).astype(BF16)
    return (kv_cache, normed_grad, weight_grad)


def solution(mesh):
    ny = 4
    nz = mesh.shape["dp"] // ny
    nx = mesh.shape["tensor"] // 2
    torus = Mesh(
        mesh.devices.reshape(mesh.shape["role"], nz, ny, nx, 2), ("role", "zl", "y", "x", "core")
    )
    placed = (
        P(ROWS, TENSOR),
        P(TENSOR),
        P(TENSOR),
        P(ROWS, TENSOR),
        P(ROWS, None),
        P(ROWS),
        P(ROWS),
        P(ROWS, TENSOR),
        P(ROWS, None),
    )
    return jax.shard_map(
        shards,
        mesh=torus,
        in_specs=placed,
        out_specs=(P(ROWS, None, TENSOR), P(ROWS, TENSOR), P(ROWS, TENSOR)),
        check_vma=False,
    )
```

```python
import jax
import jax.numpy as jnp
from jax import lax
from jax.experimental import pallas as pl
from jax.experimental.pallas import tpu as pltpu
from jax.sharding import Mesh, PartitionSpec as P

HD = 128
PAGE = 128
EPSILON = 1e-06
ROPE_BASE = 1000000.0

Z = ("role", "zl")
ROWS = ("role", "zl", "y")
DP = ("zl", "y")
TENSOR = ("x", "core")

CHUNKS = ((0, 64), (64, 64))
ORDER = ((0, False), (1, False), (0, True), (1, True))
F32 = jnp.float32
BF16 = jnp.bfloat16


def ring(size, step):
    return [(i, (i + step) % size) for i in range(size)]


def shift(value, axis, size, step):
    return lax.ppermute(value, axis, ring(size, step))


def after(value, *earlier):
    return lax.optimization_barrier((value, earlier))[0]


def by_index(blocks, index):
    size = len(blocks)
    twice = jnp.stack(blocks + blocks[:-1])
    return lax.dynamic_slice_in_dim(twice, (size - index) % size, size, 0)


def unwritten(shape, dtype):
    return pl.pallas_call(
        lambda out_ref: None,
        out_specs=pl.BlockSpec(memory_space=pl.ANY),
        out_shape=jax.ShapeDtypeStruct(shape, dtype),
    )()


def gather_weight(weight):
    ny, y = lax.axis_size("y"), lax.axis_index("y")
    line = by_index([weight] + [shift(weight, "y", ny, -s) for s in range(1, ny)], y)
    line = line.reshape(-1, weight.shape[1])
    return lax.all_gather(line, Z, axis=0, tiled=False), line


VMEM = pl.BlockSpec(memory_space=pltpu.VMEM)
FINISH_FLOPS = 40 * 10**9
SMEM = pl.BlockSpec(memory_space=pltpu.SMEM)


def project(scaled, weight, place, other=None):
    pages, part, depth = scaled.shape
    heads, cols, _ = weight.shape
    heads //= 2
    rows = pages * part

    def kernel(place_ref, scaled_ref, weight_ref, *refs):
        rows_in = scaled_ref[...].reshape(rows, depth)
        for h in range(heads):
            head = lax.rem(place_ref[0] + h, heads)
            total = lax.dot_general(
                rows_in, weight_ref[2 * head + place_ref[1]], (((1,), (1,)), ((), ())),
                preferred_element_type=F32,
            )
            if other is None:
                refs[0][head] = total.astype(BF16)
            else:
                refs[1 + h][...] = (total + refs[0][head].astype(F32)).astype(BF16)

    if other is None:
        out_specs, out_shape = VMEM, jax.ShapeDtypeStruct((heads, rows, cols), BF16)
    else:
        out_specs = [VMEM] * heads
        out_shape = [jax.ShapeDtypeStruct((rows, cols), BF16)] * heads
    args = [place, scaled, weight] + ([] if other is None else [other])
    return pl.pallas_call(
        kernel,
        in_specs=[SMEM] + [VMEM] * (len(args) - 1),
        out_specs=out_specs,
        out_shape=out_shape,
        compiler_params=pltpu.CompilerParams(vmem_limit_bytes=24 * 2**20),
        cost_estimate=pl.CostEstimate(
            flops=2 * rows * depth * cols * heads,
            bytes_accessed=2 * (rows * depth + heads * cols * (depth + rows)),
            transcendentals=0,
        ),
    )(*args)


def finish(parts, inverse, turn, bias, target, fill, start, slots):
    pages, part, cols = parts[0].shape
    half = HD // 2

    def kernel(target_ref, fill_ref, inverse_ref, turn_ref, bias_ref, *refs):
        part_refs, out_ref = refs[:-1], refs[-1]
        out_ref[...] = jnp.zeros_like(out_ref)
        bias_row = bias_ref[...].astype(F32)
        offset = lax.broadcasted_iota(jnp.int32, (part, HD), 0) + start
        low = lax.broadcasted_iota(jnp.int32, (part, HD), 1) < half

        @pl.loop(0, pages)
        def _(page):
            total = part_refs[0][page].astype(F32)
            for part_ref in part_refs[1:]:
                total = total + part_ref[page].astype(F32)
            scale, turn = inverse_ref[page], turn_ref[page]
            swapped = pltpu.roll(turn, half, 1)
            key = total[:, :HD] * scale + bias_row[:, :HD]
            value = total[:, HD:] * scale + bias_row[:, HD:]
            key = key * jnp.where(low, turn, swapped) + pltpu.roll(key, half, 1) * jnp.where(
                low, -swapped, turn
            )
            live = offset < fill_ref[page]
            where = target_ref[page]
            out_ref[where, :, :HD] = jnp.where(live, key, 0.0).astype(BF16)
            out_ref[where, :, HD:] = jnp.where(live, value, 0.0).astype(BF16)

    return pl.pallas_call(
        kernel,
        in_specs=[SMEM, SMEM] + [VMEM] * (3 + len(parts)),
        out_specs=VMEM,
        out_shape=jax.ShapeDtypeStruct((slots, part, cols), BF16),
        compiler_params=pltpu.CompilerParams(vmem_limit_bytes=24 * 2**20),
        cost_estimate=pl.CostEstimate(
            flops=FINISH_FLOPS,
            bytes_accessed=2 * part * cols * (len(parts) * pages + slots) + 8 * pages * part * HD,
            transcendentals=0,
        ),
    )(target, fill, inverse, turn, bias, *parts)


def shards(
    kv_weight,
    kv_bias,
    norm_gain,
    page_states,
    page_replica,
    page_pos,
    page_fill,
    learn_normed,
    learn_cot,
):
    nz, ny, nx = lax.axis_size(Z), lax.axis_size("y"), lax.axis_size("x")
    core, x, y, z = (lax.axis_index(name) for name in ("core", "x", "y", Z))
    pages = page_fill.shape[0]
    depth = page_states.shape[1]
    feature_count = depth * lax.axis_size(TENSOR)
    rows = kv_weight.shape[0]

    tokens = learn_cot.shape[0]
    half = HD // 2
    replicas = lax.axis_size(DP)
    capacity = max(2, 2 * pages // replicas)
    slots = replicas * capacity

    weight, line = gather_weight(kv_weight)

    cot = after(learn_cot, line).reshape(tokens, nz, ny, rows).transpose(0, 2, 1, 3)
    terms = lax.dot_general(
        cot.reshape(tokens, -1), learn_normed, (((0,), (0,)), ((), ())), preferred_element_type=F32
    ).astype(BF16)
    terms = lax.psum_scatter(terms, "y", scatter_dimension=0, tiled=True)

    states, gain, place, owners = after(
        (page_states, norm_gain, page_pos, page_replica[:, 0]), line
    )
    widened = states.astype(F32)
    scaled = (widened * gain.astype(F32)[None, :]).astype(BF16).reshape(pages, PAGE, depth)
    squares = jnp.sum(widened * widened, axis=1).reshape(pages, PAGE)
    squares = squares + shift(squares, "core", 2, 1)
    squares = squares + shift(squares, "x", nx, 1) + shift(squares, "x", nx, 2) + shift(squares, "x", nx, 3)
    inverse = lax.rsqrt(squares / feature_count + EPSILON)
    inverse = jnp.broadcast_to(inverse[:, :, None], (pages, PAGE, HD))

    exponent = jnp.arange(half, dtype=F32) * (2.0 / HD)
    frequency = jnp.power(F32(ROPE_BASE), -exponent)
    positions = place[:, None] * PAGE + jnp.arange(PAGE, dtype=jnp.int32)[None, :]
    angles = positions.astype(F32)[:, :, None] * frequency[None, None, :]
    turn = jnp.concatenate([jnp.cos(angles), jnp.sin(angles)], axis=2)

    def in_chunks(value):
        return [value[:, start : start + part] for start, part in CHUNKS]

    scaled, inverse, turn = in_chunks(scaled), in_chunks(inverse), in_chunks(turn)

    earlier = jnp.arange(pages)[None, :] < jnp.arange(pages)[:, None]
    same = owners[:, None] == owners[None, :]
    rank = jnp.sum(jnp.where(same & earlier, 1, 0), axis=1).astype(jnp.int32)
    target = owners * capacity + rank

    weight, scaled, inverse, turn, target = lax.optimization_barrier(
        (weight, scaled, inverse, turn, target)
    )
    weight_grad = lax.psum_scatter(terms, Z, scatter_dimension=0, tiled=True)

    own, far = jnp.stack([x, core]), jnp.stack([x, 1 - core])
    away, mine, last = {}, {}, None
    for c, adds in ORDER:
        rows_in = scaled[c] if last is None else after(scaled[c], last)
        if adds:
            last = mine[c] = project(rows_in, weight, own, away[c])
        else:
            last = project(rows_in, weight, far)
            away[c] = shift(last, "core", 2, 1)

    kv_cache = unwritten((slots, PAGE, 2 * HD), BF16)
    for c, chunk in enumerate(CHUNKS):
        start, part = chunk
        parts = [m if s == 0 else shift(m, "x", nx, s) for s, m in enumerate(mine[c])]
        parts = [p.reshape(pages, part, 2 * HD) for p in parts]
        placed = finish(
            parts, inverse[c], turn[c], kv_bias[None, :], target, page_fill, start, slots
        )
        if c == 0:
            placed = after(placed, mine[len(CHUNKS) - 1])
        else:
            placed = after(placed, piece)
        if c == len(CHUNKS) - 1:
            placed = after(placed, weight_grad)
        piece = lax.all_to_all(placed, DP, 0, 0, tiled=True)
        kv_cache = lax.dynamic_update_slice(kv_cache, piece, (0, start, 0))

    learn_cot, _ = lax.optimization_barrier((learn_cot, placed))
    normed_grad = jnp.dot(
        learn_cot, weight.reshape(-1, depth), preferred_element_type=F32
    ).astype(BF16)
    return (kv_cache, normed_grad, weight_grad.astype(F32))


def solution(mesh):
    ny = 4
    nz = mesh.shape["dp"] // ny
    nx = mesh.shape["tensor"] // 2
    torus = Mesh(
        mesh.devices.reshape(mesh.shape["role"], nz, ny, nx, 2), ("role", "zl", "y", "x", "core")
    )
    placed = (
        P(ROWS, TENSOR),
        P(TENSOR),
        P(TENSOR),
        P(ROWS, TENSOR),
        P(ROWS, None),
        P(ROWS),
        P(ROWS),
        P(ROWS, TENSOR),
        P(ROWS, None),
    )
    return jax.shard_map(
        shards,
        mesh=torus,
        in_specs=placed,
        out_specs=(P(ROWS, None, TENSOR), P(ROWS, TENSOR), P(ROWS, TENSOR)),
        check_vma=False,
    )
```

```python
import jax
import jax.numpy as jnp
from jax import lax
from jax.experimental import pallas as pl
from jax.experimental.pallas import tpu as pltpu
from jax.sharding import Mesh, PartitionSpec as P

HD = 128
PAGE = 128
EPSILON = 1e-06
ROPE_BASE = 1000000.0

Z = ("role", "zl")
ROWS = ("role", "zl", "y")
DP = ("zl", "y")
TENSOR = ("x", "core")

CHUNKS = ((0, 48), (48, 80))
ORDER = ((0, False), (0, True), (1, False), (1, True))
F32 = jnp.float32
BF16 = jnp.bfloat16


def ring(size, step):
    return [(i, (i + step) % size) for i in range(size)]


def shift(value, axis, size, step):
    return lax.ppermute(value, axis, ring(size, step))


def after(value, *earlier):
    return lax.optimization_barrier((value, earlier))[0]


def by_index(blocks, index):
    size = len(blocks)
    twice = jnp.stack(blocks + blocks[:-1])
    return lax.dynamic_slice_in_dim(twice, (size - index) % size, size, 0)


def unwritten(shape, dtype):
    return pl.pallas_call(
        lambda out_ref: None,
        out_specs=pl.BlockSpec(memory_space=pl.ANY),
        out_shape=jax.ShapeDtypeStruct(shape, dtype),
    )()


def gather_weight(weight):
    ny, y = lax.axis_size("y"), lax.axis_index("y")
    line = by_index([weight] + [shift(weight, "y", ny, -s) for s in range(1, ny)], y)
    line = line.reshape(-1, weight.shape[1])
    return lax.all_gather(line, Z, axis=0, tiled=False), line


VMEM = pl.BlockSpec(memory_space=pltpu.VMEM)
FINISH_FLOPS = 40 * 10**9
SMEM = pl.BlockSpec(memory_space=pltpu.SMEM)


def project(scaled, weight, place, other=None):
    pages, part, depth = scaled.shape
    heads, cols, _ = weight.shape
    heads //= 2
    rows = pages * part

    def kernel(place_ref, scaled_ref, weight_ref, *refs):
        rows_in = scaled_ref[...].reshape(rows, depth)
        for h in range(heads):
            head = lax.rem(place_ref[0] + h, heads)
            total = lax.dot_general(
                rows_in, weight_ref[2 * head + place_ref[1]], (((1,), (1,)), ((), ())),
                preferred_element_type=F32,
            )
            if other is None:
                refs[0][head] = total.astype(BF16)
            else:
                refs[1 + h][...] = (total + refs[0][head].astype(F32)).astype(BF16)

    if other is None:
        out_specs, out_shape = VMEM, jax.ShapeDtypeStruct((heads, rows, cols), BF16)
    else:
        out_specs = [VMEM] * heads
        out_shape = [jax.ShapeDtypeStruct((rows, cols), BF16)] * heads
    args = [place, scaled, weight] + ([] if other is None else [other])
    return pl.pallas_call(
        kernel,
        in_specs=[SMEM] + [VMEM] * (len(args) - 1),
        out_specs=out_specs,
        out_shape=out_shape,
        compiler_params=pltpu.CompilerParams(vmem_limit_bytes=24 * 2**20),
        cost_estimate=pl.CostEstimate(
            flops=2 * rows * depth * cols * heads,
            bytes_accessed=2 * (rows * depth + heads * cols * (depth + rows)),
            transcendentals=0,
        ),
    )(*args)


def finish(parts, inverse, turn, bias, target, fill, start, slots):
    pages, part, cols = parts[0].shape
    half = HD // 2

    def kernel(target_ref, fill_ref, inverse_ref, turn_ref, bias_ref, *refs):
        part_refs, out_ref = refs[:-1], refs[-1]
        out_ref[...] = jnp.zeros_like(out_ref)
        bias_row = bias_ref[...].astype(F32)
        offset = lax.broadcasted_iota(jnp.int32, (part, HD), 0) + start
        low = lax.broadcasted_iota(jnp.int32, (part, HD), 1) < half

        @pl.loop(0, pages)
        def _(page):
            total = part_refs[0][page].astype(F32)
            for part_ref in part_refs[1:]:
                total = total + part_ref[page].astype(F32)
            scale, turn = inverse_ref[page], turn_ref[page]
            swapped = pltpu.roll(turn, half, 1)
            key = total[:, :HD] * scale + bias_row[:, :HD]
            value = total[:, HD:] * scale + bias_row[:, HD:]
            key = key * jnp.where(low, turn, swapped) + pltpu.roll(key, half, 1) * jnp.where(
                low, -swapped, turn
            )
            live = offset < fill_ref[page]
            where = target_ref[page]
            out_ref[where, :, :HD] = jnp.where(live, key, 0.0).astype(BF16)
            out_ref[where, :, HD:] = jnp.where(live, value, 0.0).astype(BF16)

    return pl.pallas_call(
        kernel,
        in_specs=[SMEM, SMEM] + [VMEM] * (3 + len(parts)),
        out_specs=VMEM,
        out_shape=jax.ShapeDtypeStruct((slots, part, cols), BF16),
        compiler_params=pltpu.CompilerParams(vmem_limit_bytes=24 * 2**20),
        cost_estimate=pl.CostEstimate(
            flops=FINISH_FLOPS,
            bytes_accessed=2 * part * cols * (len(parts) * pages + slots) + 8 * pages * part * HD,
            transcendentals=0,
        ),
    )(target, fill, inverse, turn, bias, *parts)


def shards(
    kv_weight,
    kv_bias,
    norm_gain,
    page_states,
    page_replica,
    page_pos,
    page_fill,
    learn_normed,
    learn_cot,
):
    nz, ny, nx = lax.axis_size(Z), lax.axis_size("y"), lax.axis_size("x")
    core, x, y, z = (lax.axis_index(name) for name in ("core", "x", "y", Z))
    pages = page_fill.shape[0]
    depth = page_states.shape[1]
    feature_count = depth * lax.axis_size(TENSOR)
    rows = kv_weight.shape[0]

    tokens = learn_cot.shape[0]
    half = HD // 2
    replicas = lax.axis_size(DP)
    capacity = max(2, 2 * pages // replicas)
    slots = replicas * capacity

    weight, line = gather_weight(kv_weight)

    cot = after(learn_cot, line).reshape(tokens, nz, ny, rows).transpose(0, 2, 1, 3)
    terms = lax.dot_general(
        cot.reshape(tokens, -1), learn_normed, (((0,), (0,)), ((), ())), preferred_element_type=F32
    ).astype(BF16)
    terms = lax.psum_scatter(terms, "y", scatter_dimension=0, tiled=True)

    states, gain, place, owners = after(
        (page_states, norm_gain, page_pos, page_replica[:, 0]), line
    )
    widened = states.astype(F32)
    by_page = states.reshape(pages, PAGE, depth)
    scaled = [
        (by_page[:, start : start + part].astype(F32) * gain.astype(F32)[None, None, :]).astype(BF16)
        for start, part in CHUNKS
    ]
    squares = jnp.sum(widened * widened, axis=1).reshape(pages, PAGE)
    squares = squares + shift(squares, "core", 2, 1)
    squares = squares + shift(squares, "x", nx, 1) + shift(squares, "x", nx, 2) + shift(squares, "x", nx, 3)
    inverse = lax.rsqrt(squares / feature_count + EPSILON)

    exponent = jnp.arange(half, dtype=F32) * (2.0 / HD)
    frequency = jnp.power(F32(ROPE_BASE), -exponent)
    positions = place[:, None] * PAGE + jnp.arange(PAGE, dtype=jnp.int32)[None, :]
    angles = positions.astype(F32)[:, :, None] * frequency[None, None, :]
    turn = jnp.concatenate([jnp.cos(angles), jnp.sin(angles)], axis=2)

    def in_chunks(value):
        return [value[:, start : start + part] for start, part in CHUNKS]

    turn = in_chunks(turn)

    earlier = jnp.arange(pages)[None, :] < jnp.arange(pages)[:, None]
    same = owners[:, None] == owners[None, :]
    rank = jnp.sum(jnp.where(same & earlier, 1, 0), axis=1).astype(jnp.int32)
    target = owners * capacity + rank

    weight, scaled, inverse, turn, target = lax.optimization_barrier(
        (weight, scaled, inverse, turn, target)
    )
    weight_grad = lax.psum_scatter(terms, Z, scatter_dimension=0, tiled=True)

    inverse = in_chunks(jnp.broadcast_to(inverse[:, :, None], (pages, PAGE, HD)))
    own, far = jnp.stack([x, core]), jnp.stack([x, 1 - core])
    away, mine, last = {}, {}, None
    for c, adds in ORDER:
        rows_in = scaled[c] if last is None else after(scaled[c], last)
        if adds:
            last = mine[c] = project(rows_in, weight, own, away[c])
        else:
            last = project(rows_in, weight, far)
            away[c] = shift(last, "core", 2, 1)

    kv_cache = unwritten((slots, PAGE, 2 * HD), BF16)
    for c, chunk in enumerate(CHUNKS):
        start, part = chunk
        parts = [m if s == 0 else shift(m, "x", nx, s) for s, m in enumerate(mine[c])]
        parts = [p.reshape(pages, part, 2 * HD) for p in parts]
        placed = finish(
            parts, inverse[c], turn[c], kv_bias[None, :], target, page_fill, start, slots
        )
        if c == 0:
            placed = after(placed, mine[len(CHUNKS) - 1], inverse[1:])
        else:
            placed = after(placed, piece)
        if c == len(CHUNKS) - 1:
            placed = after(placed, weight_grad)
        piece = lax.all_to_all(placed, DP, 0, 0, tiled=True)
        kv_cache = lax.dynamic_update_slice(kv_cache, piece, (0, start, 0))

    learn_cot, _ = lax.optimization_barrier((learn_cot, placed))
    normed_grad = jnp.dot(
        learn_cot, weight.reshape(-1, depth), preferred_element_type=F32
    ).astype(BF16)
    return (kv_cache, normed_grad, weight_grad.astype(F32))


def solution(mesh):
    ny = 4
    nz = mesh.shape["dp"] // ny
    nx = mesh.shape["tensor"] // 2
    torus = Mesh(
        mesh.devices.reshape(mesh.shape["role"], nz, ny, nx, 2), ("role", "zl", "y", "x", "core")
    )
    placed = (
        P(ROWS, TENSOR),
        P(TENSOR),
        P(TENSOR),
        P(ROWS, TENSOR),
        P(ROWS, None),
        P(ROWS),
        P(ROWS),
        P(ROWS, TENSOR),
        P(ROWS, None),
    )
    return jax.shard_map(
        shards,
        mesh=torus,
        in_specs=placed,
        out_specs=(P(ROWS, None, TENSOR), P(ROWS, TENSOR), P(ROWS, TENSOR)),
        check_vma=False,
    )
```

```python
import jax
import jax.numpy as jnp
from jax import lax
from jax.experimental import pallas as pl
from jax.experimental.pallas import tpu as pltpu
from jax.sharding import Mesh, PartitionSpec as P

HD = 128
PAGE = 128
EPSILON = 1e-06
ROPE_BASE = 1000000.0

Z = ("role", "zl")
ROWS = ("role", "zl", "y")
DP = ("zl", "y")
TENSOR = ("x", "core")

CHUNKS = ((0, 48), (48, 80))
ORDER = ((0, False), (0, True), (1, False), (1, True))
F32 = jnp.float32
BF16 = jnp.bfloat16


def ring(size, step):
    return [(i, (i + step) % size) for i in range(size)]


def shift(value, axis, size, step):
    return lax.ppermute(value, axis, ring(size, step))


def after(value, *earlier):
    return lax.optimization_barrier((value, earlier))[0]


def by_index(blocks, index):
    size = len(blocks)
    twice = jnp.stack(blocks + blocks[:-1])
    return lax.dynamic_slice_in_dim(twice, (size - index) % size, size, 0)


def unwritten(shape, dtype):
    return pl.pallas_call(
        lambda out_ref: None,
        out_specs=pl.BlockSpec(memory_space=pl.ANY),
        out_shape=jax.ShapeDtypeStruct(shape, dtype),
    )()


def gather_weight(weight):
    ny, y = lax.axis_size("y"), lax.axis_index("y")
    line = by_index([weight] + [shift(weight, "y", ny, -s) for s in range(1, ny)], y)
    line = line.reshape(-1, weight.shape[1])
    return lax.all_gather(line, Z, axis=0, tiled=False), line


VMEM = pl.BlockSpec(memory_space=pltpu.VMEM)
FINISH_FLOPS = 40 * 10**9
SMEM = pl.BlockSpec(memory_space=pltpu.SMEM)


def project(scaled, weight, place, other=None):
    pages, part, depth = scaled.shape
    heads, cols, _ = weight.shape
    heads //= 2
    rows = pages * part

    def kernel(place_ref, scaled_ref, weight_ref, *refs):
        rows_in = scaled_ref[...].reshape(rows, depth)
        for h in range(heads):
            head = lax.rem(place_ref[0] + h, heads)
            total = lax.dot_general(
                rows_in, weight_ref[2 * head + place_ref[1]], (((1,), (1,)), ((), ())),
                preferred_element_type=F32,
            )
            if other is None:
                refs[0][head] = total.astype(BF16)
            else:
                refs[1 + h][...] = (total + refs[0][head].astype(F32)).astype(BF16)

    if other is None:
        out_specs, out_shape = VMEM, jax.ShapeDtypeStruct((heads, rows, cols), BF16)
    else:
        out_specs = [VMEM] * heads
        out_shape = [jax.ShapeDtypeStruct((rows, cols), BF16)] * heads
    args = [place, scaled, weight] + ([] if other is None else [other])
    return pl.pallas_call(
        kernel,
        in_specs=[SMEM] + [VMEM] * (len(args) - 1),
        out_specs=out_specs,
        out_shape=out_shape,
        compiler_params=pltpu.CompilerParams(vmem_limit_bytes=24 * 2**20),
        cost_estimate=pl.CostEstimate(
            flops=2 * rows * depth * cols * heads,
            bytes_accessed=2 * (rows * depth + heads * cols * (depth + rows)),
            transcendentals=0,
        ),
    )(*args)


def finish(parts, inverse, turn, bias, target, fill, start, slots):
    pages, part, cols = parts[0].shape
    half = HD // 2

    def kernel(target_ref, fill_ref, inverse_ref, turn_ref, bias_ref, *refs):
        part_refs, out_ref = refs[:-1], refs[-1]
        out_ref[...] = jnp.zeros_like(out_ref)
        bias_row = bias_ref[...].astype(F32)
        offset = lax.broadcasted_iota(jnp.int32, (part, HD), 0) + start
        low = lax.broadcasted_iota(jnp.int32, (part, HD), 1) < half

        @pl.loop(0, pages)
        def _(page):
            total = part_refs[0][page].astype(F32)
            for part_ref in part_refs[1:]:
                total = total + part_ref[page].astype(F32)
            scale, turn = inverse_ref[page], turn_ref[page]
            swapped = pltpu.roll(turn, half, 1)
            key = total[:, :HD] * scale + bias_row[:, :HD]
            value = total[:, HD:] * scale + bias_row[:, HD:]
            key = key * jnp.where(low, turn, swapped) + pltpu.roll(key, half, 1) * jnp.where(
                low, -swapped, turn
            )
            live = offset < fill_ref[page]
            where = target_ref[page]
            out_ref[where, :, :HD] = jnp.where(live, key, 0.0).astype(BF16)
            out_ref[where, :, HD:] = jnp.where(live, value, 0.0).astype(BF16)

    return pl.pallas_call(
        kernel,
        in_specs=[SMEM, SMEM] + [VMEM] * (3 + len(parts)),
        out_specs=VMEM,
        out_shape=jax.ShapeDtypeStruct((slots, part, cols), BF16),
        compiler_params=pltpu.CompilerParams(vmem_limit_bytes=24 * 2**20),
        cost_estimate=pl.CostEstimate(
            flops=FINISH_FLOPS,
            bytes_accessed=2 * part * cols * (len(parts) * pages + slots) + 8 * pages * part * HD,
            transcendentals=0,
        ),
    )(target, fill, inverse, turn, bias, *parts)


def shards(
    kv_weight,
    kv_bias,
    norm_gain,
    page_states,
    page_replica,
    page_pos,
    page_fill,
    learn_normed,
    learn_cot,
):
    nz, ny, nx = lax.axis_size(Z), lax.axis_size("y"), lax.axis_size("x")
    core, x, y, z = (lax.axis_index(name) for name in ("core", "x", "y", Z))
    pages = page_fill.shape[0]
    depth = page_states.shape[1]
    feature_count = depth * lax.axis_size(TENSOR)
    rows = kv_weight.shape[0]

    tokens = learn_cot.shape[0]
    half = HD // 2
    replicas = lax.axis_size(DP)
    capacity = max(2, 2 * pages // replicas)
    slots = replicas * capacity

    weight, line = gather_weight(kv_weight)

    cot = after(learn_cot, line).reshape(tokens, nz, ny, rows).transpose(0, 2, 1, 3)
    terms = lax.dot_general(
        cot.reshape(tokens, -1), learn_normed, (((0,), (0,)), ((), ())), preferred_element_type=F32
    ).astype(BF16)
    terms = lax.psum_scatter(terms, "y", scatter_dimension=0, tiled=True)

    states, gain, place, owners = after(
        (page_states, norm_gain, page_pos, page_replica[:, 0]), line
    )
    widened = states.astype(F32)
    by_page = states.reshape(pages, PAGE, depth)
    scaled = [
        (by_page[:, start : start + part].astype(F32) * gain.astype(F32)[None, None, :]).astype(BF16)
        for start, part in CHUNKS
    ]
    squares = jnp.sum(widened * widened, axis=1).reshape(pages, PAGE)
    squares = squares + shift(squares, "core", 2, 1)
    squares = squares + shift(squares, "x", nx, 1) + shift(squares, "x", nx, 2) + shift(squares, "x", nx, 3)
    inverse = lax.rsqrt(squares / feature_count + EPSILON)

    exponent = jnp.arange(half, dtype=F32) * (2.0 / HD)
    frequency = jnp.power(F32(ROPE_BASE), -exponent)
    positions = place[:, None] * PAGE + jnp.arange(PAGE, dtype=jnp.int32)[None, :]
    angles = positions.astype(F32)[:, :, None] * frequency[None, None, :]
    turn = jnp.concatenate([jnp.cos(angles), jnp.sin(angles)], axis=2)

    def in_chunks(value):
        return [value[:, start : start + part] for start, part in CHUNKS]

    turn = in_chunks(turn)

    earlier = jnp.arange(pages)[None, :] < jnp.arange(pages)[:, None]
    same = owners[:, None] == owners[None, :]
    rank = jnp.sum(jnp.where(same & earlier, 1, 0), axis=1).astype(jnp.int32)
    target = owners * capacity + rank

    weight, scaled, inverse, turn, target = lax.optimization_barrier(
        (weight, scaled, inverse, turn, target)
    )
    weight_grad = lax.psum_scatter(terms, Z, scatter_dimension=0, tiled=True)

    inverse = in_chunks(jnp.broadcast_to(inverse[:, :, None], (pages, PAGE, HD)))
    own, far = jnp.stack([x, core]), jnp.stack([x, 1 - core])
    away, mine, last = {}, {}, None
    for c, adds in ORDER:
        rows_in = scaled[c] if last is None else after(scaled[c], last)
        if adds:
            last = mine[c] = project(rows_in, weight, own, away[c])
        else:
            last = project(rows_in, weight, far)
            away[c] = shift(last, "core", 2, 1)

    kv_cache = unwritten((slots, PAGE, 2 * HD), BF16)
    for c, chunk in enumerate(CHUNKS):
        start, part = chunk
        parts = [m if s == 0 else shift(m, "x", nx, s) for s, m in enumerate(mine[c])]
        parts = [p.reshape(pages, part, 2 * HD) for p in parts]
        placed = finish(
            parts, inverse[c], turn[c], kv_bias[None, :], target, page_fill, start, slots
        )
        if c == 0:
            placed = after(placed, inverse[1:])
        else:
            placed = after(placed, piece)
        if c == len(CHUNKS) - 1:
            placed = after(placed, weight_grad)
        piece = lax.all_to_all(placed, DP, 0, 0, tiled=True)
        kv_cache = lax.dynamic_update_slice(kv_cache, piece, (0, start, 0))

    learn_cot, _ = lax.optimization_barrier((learn_cot, placed))
    normed_grad = jnp.dot(
        learn_cot, weight.reshape(-1, depth), preferred_element_type=F32
    ).astype(BF16)
    return (kv_cache, normed_grad, weight_grad.astype(F32))


def solution(mesh):
    ny = 4
    nz = mesh.shape["dp"] // ny
    nx = mesh.shape["tensor"] // 2
    torus = Mesh(
        mesh.devices.reshape(mesh.shape["role"], nz, ny, nx, 2), ("role", "zl", "y", "x", "core")
    )
    placed = (
        P(ROWS, TENSOR),
        P(TENSOR),
        P(TENSOR),
        P(ROWS, TENSOR),
        P(ROWS, None),
        P(ROWS),
        P(ROWS),
        P(ROWS, TENSOR),
        P(ROWS, None),
    )
    return jax.shard_map(
        shards,
        mesh=torus,
        in_specs=placed,
        out_specs=(P(ROWS, None, TENSOR), P(ROWS, TENSOR), P(ROWS, TENSOR)),
        check_vma=False,
    )
```
